32 devices in a mesh: expert: 8 (over y, x, core), hidden: 4 (over z).
Axes of the slice: x: 2, y: 2, z: 4, core: 2. Of those that a mesh axis runs over, the one named last changes fastest.
Arguments:
- tokens: bfloat16 [6272, 768], P(('expert', 'hidden')), may hold values from -512 to 512
- out_grad: bfloat16 [6272, 768], P(('expert', 'hidden')), may hold values from -12 to 12
- slot_router: bfloat16 [768, 32], replicated, may hold values from -0.5 to 0.5
- weight_in: bfloat16 [16, 768, 3072], P('expert', None, 'hidden'), may hold values from -0.21875 to 0.21875
- weight_out: bfloat16 [16, 3072, 768], P('expert', 'hidden'), may hold values from -0.109375 to 0.109375
Outputs:
- token_grad: bfloat16 [6272, 768], P(('expert', 'hidden'))
- router_grad: float32 [768, 32], P('hidden', 'expert')
- weight_in_grad: bfloat16 [16, 768, 3072], P('expert', None, 'hidden')
- weight_out_grad: bfloat16 [16, 3072, 768], P('expert', 'hidden')
The draws below stay inside these ranges and needn't reach their ends.
All inputs are finite; a program needn't handle non-finite values.
Results may differ from the reference program's by a relative error of at most 0.019.
Values may be sent and summed in bfloat16 or wider, within the bound.
No kernel may reach another device: no remote copies, remote signals or barrier semaphores. Data moves between devices by JAX's collectives and lax.ppermute only.
A program may use at most 64 MiB of HBM per device.

```python
import jax
import jax.numpy as jnp
from jax import lax

D = 768
FF = 3072
SLOTS = 2
TOK = 196
EXPERTS = 16
IMAGES = 32
ROWS = 6272
N_HIDDEN = 4


def router_values(key):
    raw_values = jax.random.normal(jax.random.fold_in(key, 11), (D, EXPERTS * SLOTS), jnp.float32)
    return 0.08 * jnp.clip(raw_values, -6.0, 6.0)


def draw_slot_router(key, part):
    return router_values(key).astype(jnp.bfloat16)


def draw_tokens(key, part):
    base_values = jnp.clip(jax.random.normal(jax.random.fold_in(key, 21), (IMAGES, TOK, D), jnp.float32), -6.0, 6.0)
    return base_values.reshape(IMAGES * TOK, D).astype(jnp.bfloat16)


def levels(own_key, shape, split, low, top_value):
    def one(dim, blocks):
        draws = jax.random.uniform(jax.random.fold_in(jax.random.fold_in(own_key, 6), dim), (blocks,), jnp.float32, low / len(split), top_value / len(split))
        return jnp.repeat(jnp.exp(draws), shape[dim] // blocks).reshape((-1,) + (1,) * (len(shape) - dim - 1))

    gain = one(*split[0])
    for cut in split[1:]:
        gain = gain * one(*cut)
    return gain


def bell_draw(key, shape, scale, most, cuts=(), dtype=jnp.bfloat16):
    gain = levels(key, shape, cuts, -0.22, 0.18) if cuts else 1.0
    values = jax.random.normal(key, shape, jnp.float32) * scale * gain
    return jnp.minimum(jnp.maximum(values, -most), most).astype(dtype)


def setup_inputs(seed: int = 0) -> dict:
    key_of = jax.random.split(jax.random.key(seed), 6)
    tokens = draw_tokens(jax.random.fold_in(key_of[5], 71), 0)
    out_grad = bell_draw(key_of[1], (ROWS, D), 2.0, 12.0, ((0, 32),))
    slot_router = draw_slot_router(jax.random.fold_in(key_of[5], 71), 0)
    weight_in = bell_draw(key_of[3], (EXPERTS, D, FF), D ** -0.5, 0.21875, ((0, 8), (2, 4)))
    weight_out = bell_draw(key_of[4], (EXPERTS, FF, D), FF ** -0.5, 0.109375, ((0, 8), (1, 4)))
    return dict(tokens=tokens, out_grad=out_grad, slot_router=slot_router, weight_in=weight_in, weight_out=weight_out)


def gelu_value(values):
    return 0.5 * values * (1.0 + lax.erf(values * 0.7071067811865476))


def gelu_slope(values):
    return 0.5 * (1.0 + lax.erf(values * 0.7071067811865476)) + values * jnp.exp(-0.5 * values * values) * 0.3989422804014327


def reference(tokens, out_grad, slot_router, weight_in, weight_out):
    high = lax.Precision.HIGHEST
    images = tokens.shape[0] // TOK
    experts = weight_in.shape[0]
    inputs = tokens.reshape(images, TOK, D)
    out_grads = out_grad.reshape(images, TOK, D)
    inputs32 = inputs.astype(jnp.float32)
    out_grads32 = out_grads.astype(jnp.float32)
    router32 = slot_router.astype(jnp.float32)
    logits = jnp.einsum('btd,dc->btc', inputs32, router32, precision=high)
    dispatch = jax.nn.softmax(logits, axis=1)
    combine = jax.nn.softmax(logits, axis=2)
    dispatch16 = dispatch.astype(jnp.bfloat16)
    combine16 = combine.astype(jnp.bfloat16)
    slot_in = jnp.einsum('btc,btd->bcd', dispatch16.astype(jnp.float32), inputs32, precision=high).astype(jnp.bfloat16)
    slot_grad = jnp.einsum('btc,btd->bcd', combine16.astype(jnp.float32), out_grads32, precision=high).astype(jnp.bfloat16)

    def by_expert(values):
        return values.reshape(images, experts, SLOTS, D).transpose(1, 0, 2, 3).reshape(experts, images * SLOTS, D)

    def back_to_images(values):
        return values.reshape(experts, images, SLOTS, D).transpose(1, 0, 2, 3).reshape(images, experts * SLOTS, D)

    quarter = FF // N_HIDDEN

    def per_expert(items):
        slot_inputs, slot_grads, w_first, w_second = items
        row_count = slot_inputs.shape[0]
        pre_act = jnp.dot(slot_inputs, w_first, preferred_element_type=jnp.float32)
        activated = gelu_value(pre_act).astype(jnp.bfloat16)
        pieces = jnp.einsum('rqf,qfd->qrd', activated.reshape(row_count, N_HIDDEN, quarter).astype(jnp.float32),
                            w_second.reshape(N_HIDDEN, quarter, D).astype(jnp.float32), precision=high)
        slot_out = jnp.sum(pieces.astype(jnp.bfloat16).astype(jnp.float32), axis=0).astype(jnp.bfloat16)
        d_act = jnp.dot(slot_grads, w_second.T, preferred_element_type=jnp.float32)
        d_pre = (d_act * gelu_slope(pre_act)).astype(jnp.bfloat16)
        grad_second = jnp.dot(activated.T, slot_grads, preferred_element_type=jnp.float32).astype(jnp.bfloat16)
        grad_first = jnp.dot(slot_inputs.T, d_pre, preferred_element_type=jnp.float32).astype(jnp.bfloat16)
        back_pieces = jnp.einsum('rqf,dqf->qrd', d_pre.reshape(row_count, N_HIDDEN, quarter).astype(jnp.float32),
                                 w_first.reshape(D, N_HIDDEN, quarter).astype(jnp.float32), precision=high)
        slot_in_grad = jnp.sum(back_pieces.astype(jnp.bfloat16).astype(jnp.float32), axis=0).astype(jnp.bfloat16)
        return slot_out, slot_in_grad, grad_first, grad_second

    slot_out, slot_in_grad, weight_in_grad, weight_out_grad = lax.map(
        per_expert, (by_expert(slot_in), by_expert(slot_grad), weight_in, weight_out))
    slot_out = back_to_images(slot_out).astype(jnp.float32)
    slot_in_grad = back_to_images(slot_in_grad).astype(jnp.float32)
    d_combine = jnp.einsum('btd,bcd->btc', out_grads32, slot_out, precision=high)
    d_dispatch = jnp.einsum('btd,bcd->btc', inputs32, slot_in_grad, precision=high)
    from_combine = combine * (d_combine - jnp.sum(combine * d_combine, axis=2, keepdims=True))
    from_dispatch = dispatch * (d_dispatch - jnp.sum(dispatch * d_dispatch, axis=1, keepdims=True))
    d_logits = (from_combine + from_dispatch).astype(jnp.bfloat16).astype(jnp.float32)
    token_grad = (jnp.einsum('btc,bcd->btd', dispatch16.astype(jnp.float32), slot_in_grad, precision=high)
                  + jnp.einsum('btc,dc->btd', d_logits, router32, precision=high)).astype(jnp.bfloat16)
    router_grad = jnp.einsum('btd,btc->dc', inputs32, d_logits, precision=high)
    return token_grad.reshape(images * TOK, D), router_grad, weight_in_grad, weight_out_grad
```

```python
import jax
import jax.numpy as jnp
from jax import lax
from jax.sharding import PartitionSpec as P

SLOTS = 2
TOK = 196
BOTH = ("expert", "hidden")


def gelu_value(values):
    return 0.5 * values * (1.0 + lax.erf(values * 0.7071067811865476))


def gelu_slope(values):
    return (
        0.5 * (1.0 + lax.erf(values * 0.7071067811865476))
        + values * jnp.exp(-0.5 * values * values) * 0.3989422804014327
    )


def exchange(blocks):
    return lax.all_to_all(blocks, BOTH, split_axis=0, concat_axis=0, tiled=True)


def per_device(n_expert, n_hidden, tokens, out_grad, slot_router, weight_in, weight_out):
    f32, bf16 = jnp.float32, jnp.bfloat16
    width = tokens.shape[1]
    images = tokens.shape[0] // TOK
    local_experts = weight_in.shape[0]
    local_slots = local_experts * SLOTS
    devices = n_expert * n_hidden
    inputs = tokens.reshape(images, TOK, width)
    out_grads = out_grad.reshape(images, TOK, width)
    logits = jnp.einsum("btd,dc->btc", inputs, slot_router, preferred_element_type=f32)
    dispatch = jax.nn.softmax(logits, axis=1)
    combine = jax.nn.softmax(logits, axis=2)
    dispatch16 = dispatch.astype(bf16)
    combine16 = combine.astype(bf16)
    slot_in = jnp.einsum("btc,btd->bcd", dispatch16, inputs, preferred_element_type=f32)
    slot_grad = jnp.einsum("btc,btd->bcd", combine16, out_grads, preferred_element_type=f32)
    slots = jnp.stack([slot_in.astype(bf16), slot_grad.astype(bf16)])
    slots = slots.reshape(2, images, n_expert, local_slots, width).transpose(2, 0, 1, 3, 4)
    sent = jnp.broadcast_to(slots[:, None], (n_expert, n_hidden) + slots.shape[1:])
    received = exchange(sent.reshape(devices, 2 * images * local_slots, width))
    received = received.reshape(devices, 2, images, local_experts, SLOTS, width)
    received = received.transpose(1, 3, 0, 2, 4, 5)
    rows = devices * images * SLOTS
    slot_inputs = received[0].reshape(local_experts, rows, width)
    slot_grads = received[1].reshape(local_experts, rows, width)
    pre_act = jnp.einsum("erd,edf->erf", slot_inputs, weight_in, preferred_element_type=f32)
    activated = gelu_value(pre_act).astype(bf16)
    forward = jnp.einsum("erf,efd->erd", activated, weight_out, preferred_element_type=f32)
    d_act = jnp.einsum("erd,efd->erf", slot_grads, weight_out, preferred_element_type=f32)
    d_pre = (d_act * gelu_slope(pre_act)).astype(bf16)
    backward = jnp.einsum("erf,edf->erd", d_pre, weight_in, preferred_element_type=f32)
    partials = jnp.stack([forward.astype(bf16), backward.astype(bf16)])
    partials = partials.reshape(2, local_experts, devices, images, SLOTS, width)
    partials = partials.transpose(2, 0, 3, 1, 4, 5)
    back = exchange(partials.reshape(devices, 2 * images * local_slots, width))
    grad_second = jnp.einsum("erf,erd->efd", activated, slot_grads, preferred_element_type=f32)
    grad_first = jnp.einsum("erd,erf->edf", slot_inputs, d_pre, preferred_element_type=f32)
    back = back.reshape(n_expert, n_hidden, 2, images, local_slots, width)
    summed = jnp.sum(back.astype(f32), axis=1).astype(bf16).transpose(1, 2, 0, 3, 4)
    summed = summed.reshape(2, images, n_expert * local_slots, width)
    slot_out, slot_in_grad = summed[0], summed[1]
    d_combine = jnp.einsum("btd,bcd->btc", out_grads, slot_out, preferred_element_type=f32)
    d_dispatch = jnp.einsum("btd,bcd->btc", inputs, slot_in_grad, preferred_element_type=f32)
    from_combine = combine * (d_combine - jnp.sum(combine * d_combine, axis=2, keepdims=True))
    from_dispatch = dispatch * (d_dispatch - jnp.sum(dispatch * d_dispatch, axis=1, keepdims=True))
    d_logits = (from_combine + from_dispatch).astype(bf16)
    token_grad = (
        jnp.einsum("btc,bcd->btd", dispatch16, slot_in_grad, preferred_element_type=f32)
        + jnp.einsum("btc,dc->btd", d_logits, slot_router, preferred_element_type=f32)
    ).astype(bf16)
    router_term = jnp.einsum("btc,btd->cd", d_logits, inputs, preferred_element_type=f32)
    router_term = router_term.reshape(n_expert, local_slots, n_hidden, width // n_hidden)
    router_term = router_term.transpose(0, 2, 1, 3)
    router_parts = exchange(router_term.reshape(devices, local_slots, width // n_hidden))
    router_grad = jnp.sum(router_parts, axis=0).T
    return (
        token_grad.reshape(images * TOK, width),
        router_grad,
        grad_first.astype(bf16),
        grad_second.astype(bf16),
    )


def solution(mesh):
    def run(*arrays):
        return per_device(mesh.shape["expert"], mesh.shape["hidden"], *arrays)

    return jax.shard_map(
        run,
        mesh=mesh,
        in_specs=(
            P(BOTH, None),
            P(BOTH, None),
            P(),
            P("expert", None, "hidden"),
            P("expert", "hidden", None),
        ),
        out_specs=(
            P(BOTH, None),
            P("hidden", "expert"),
            P("expert", None, "hidden"),
            P("expert", "hidden", None),
        ),
        check_vma=False,
    )
```

```python
import functools

import jax
import jax.numpy as jnp
from jax import lax
from jax.experimental import pallas as pl
from jax.experimental.pallas import tpu as pltpu
from jax.sharding import PartitionSpec as P

SLOTS = 2
TOK = 196
BOTH = ("expert", "hidden")
F32, BF16 = jnp.float32, jnp.bfloat16
NN = (((1,), (0,)), ((), ()))
NT = (((1,), (1,)), ((), ()))
TN = (((0,), (0,)), ((), ()))


def dot(left, right, dims=NN):
    return lax.dot_general(left, right, dims, preferred_element_type=F32)


def reorder(shape, old_axes, rows):
    out_row = lax.broadcasted_iota(jnp.int32, (rows, 1), 0)
    strides = [1] * len(shape)
    for axis in reversed(range(len(shape) - 1)):
        strides[axis] = strides[axis + 1] * shape[axis + 1]
    source = jnp.zeros_like(out_row)
    rest = out_row
    for axis in reversed(old_axes):
        source = source + lax.rem(rest, shape[axis]) * strides[axis]
        rest = lax.div(rest, shape[axis])
    columns = lax.broadcasted_iota(jnp.int32, (rows, rows), 1)
    return jnp.where(columns == source, 1.0, 0.0).astype(BF16)


def softmaxes(logits):
    by_token = jnp.exp(logits - jnp.max(logits, axis=1, keepdims=True))
    dispatch = by_token / jnp.sum(by_token, axis=1, keepdims=True)
    by_slot = jnp.exp(logits - jnp.max(logits, axis=0, keepdims=True))
    combine = by_slot / jnp.sum(by_slot, axis=0, keepdims=True)
    return dispatch, combine


def slots_kernel(dims, tokens, out_grad, router, logits_out, sent):
    n_expert, n_hidden, local_slots = dims
    images, _, width = tokens.shape
    slots = n_expert * local_slots
    order = reorder((2, n_expert, local_slots), (1, 0, 2), 2 * slots)
    for image in range(images):
        logits = dot(router[...], tokens[image], NT)
        logits_out[image] = logits
        dispatch, combine = softmaxes(logits)
        slot_in = dot(dispatch.astype(BF16), tokens[image]).astype(BF16)
        slot_grad = dot(combine.astype(BF16), out_grad[image]).astype(BF16)
        both = dot(order, jnp.concatenate([slot_in, slot_grad], axis=0)).astype(BF16)
        both = both.reshape(n_expert, 2 * local_slots, width)
        for copy in range(n_hidden):
            sent[:, copy, image] = both


def experts_kernel(dims, received, weight_in, weight_out, parts, rows_out, act_out, d_pre_out):
    images, local_experts, chunk = dims
    devices, per_source, width = received.shape
    shape = (chunk, images, 2, local_experts, SLOTS)
    size = chunk * per_source
    part = size // (2 * local_experts)
    to_expert = (2, 3, 0, 1, 4)
    order = reorder(shape, to_expert, size)
    moved = tuple(shape[axis] for axis in to_expert)
    back = reorder(moved, tuple(to_expert.index(axis) for axis in range(5)), size)
    for start in range(0, devices, chunk):
        block = received[start : start + chunk].reshape(size, width)
        rows = dot(order, block).astype(BF16)
        base = start // chunk * part
        forwards, backwards = [], []
        for expert in range(local_experts):
            slot_in = rows[expert * part : (expert + 1) * part]
            slot_grad = rows[(local_experts + expert) * part : (local_experts + expert + 1) * part]
            rows_out[0, expert, base : base + part] = slot_in
            rows_out[1, expert, base : base + part] = slot_grad
            pre = dot(slot_in, weight_in[expert])
            d_act = dot(slot_grad, weight_out[expert], NT)
            half = 0.5 * (1.0 + lax.erf(pre * 0.7071067811865476))
            act = (pre * half).astype(BF16)
            slope = half + pre * jnp.exp(-0.5 * pre * pre) * 0.3989422804014327
            d_pre = (d_act * slope).astype(BF16)
            act_out[expert, base : base + part] = act
            d_pre_out[expert, base : base + part] = d_pre
            forwards.append(dot(act, weight_out[expert]).astype(BF16))
            backwards.append(dot(d_pre, weight_in[expert], NT).astype(BF16))
        results = dot(back, jnp.concatenate(forwards + backwards, axis=0)).astype(BF16)
        parts[start : start + chunk] = results.reshape(chunk, per_source, width)


def weights_kernel(rows, act, d_pre, grad_in, grad_out):
    grad_in[0] = dot(rows[0, 0], d_pre[0], TN).astype(BF16)
    grad_out[0] = dot(act[0], rows[1, 0], TN).astype(BF16)


def images_kernel(dims, logits_in, tokens, out_grad, router, parts, token_grad, terms):
    n_expert, n_hidden, local_slots = dims
    images, _, width = tokens.shape
    slots = n_expert * local_slots
    order = reorder((n_expert, 2, local_slots), (1, 0, 2), 2 * slots)
    total = None
    for image in range(images):
        dispatch, combine = softmaxes(logits_in[image])
        summed = parts[:, 0, image].astype(F32)
        for part in range(1, n_hidden):
            summed = summed + parts[:, part, image].astype(F32)
        summed = summed.reshape(2 * slots, width).astype(BF16)
        both = dot(order, summed).astype(BF16)
        slot_out, slot_in_grad = both[:slots], both[slots:]
        d_combine = dot(slot_out, out_grad[image], NT)
        d_dispatch = dot(slot_in_grad, tokens[image], NT)
        from_combine = combine * (d_combine - jnp.sum(combine * d_combine, axis=0, keepdims=True))
        from_dispatch = dispatch * (
            d_dispatch - jnp.sum(dispatch * d_dispatch, axis=1, keepdims=True)
        )
        d_logits = (from_combine + from_dispatch).astype(BF16)
        term = dot(d_logits, tokens[image])
        total = term if total is None else total + term
        left = jnp.concatenate([dispatch.astype(BF16), d_logits], axis=0)
        right = jnp.concatenate([slot_in_grad, router[...]], axis=0)
        token_grad[image] = dot(left, right, TN).astype(BF16)
    block = width // n_hidden
    for part in range(n_hidden):
        columns = total[:, part * block : (part + 1) * block]
        terms[:, part] = columns.reshape(n_expert, local_slots, block)


def exchange(blocks):
    return lax.all_to_all(blocks, BOTH, split_axis=0, concat_axis=0, tiled=True)


def call(kernel, outs, args, flops, **more):
    moved = sum(x.size * x.dtype.itemsize for x in list(outs) + list(args))
    return pl.pallas_call(
        kernel,
        out_shape=outs,
        cost_estimate=pl.CostEstimate(flops=flops, bytes_accessed=moved, transcendentals=0),
        compiler_params=pltpu.CompilerParams(vmem_limit_bytes=40 * 2**20),
        **more,
    )(*args)


def per_device(n_expert, n_hidden, tokens, out_grad, slot_router, weight_in, weight_out):
    width = tokens.shape[1]
    images = tokens.shape[0] // TOK
    local_experts, _, hidden = weight_in.shape
    local_slots = local_experts * SLOTS
    slots = n_expert * local_slots
    devices = n_expert * n_hidden
    per_source = 2 * images * local_slots
    rows = devices * images * SLOTS
    shape = jax.ShapeDtypeStruct
    inputs = tokens.reshape(images, TOK, width)
    out_grads = out_grad.reshape(images, TOK, width)
    router = slot_router.T
    dims = (n_expert, n_hidden, local_slots)

    logits, sent = call(
        functools.partial(slots_kernel, dims),
        (
            shape((images, slots, TOK), F32),
            shape((n_expert, n_hidden, images, 2 * local_slots, width), BF16),
        ),
        (inputs, out_grads, router),
        6 * images * slots * TOK * width,
    )
    received = exchange(sent.reshape(devices, per_source, width))
    chunk = max(c for c in range(1, devices + 1) if devices % c == 0 and c * per_source <= 256)
    parts, slot_rows, act, d_pre = call(
        functools.partial(experts_kernel, (images, local_experts, chunk)),
        (
            shape((devices, per_source, width), BF16),
            shape((2, local_experts, rows, width), BF16),
            shape((local_experts, rows, hidden), BF16),
            shape((local_experts, rows, hidden), BF16),
        ),
        (received, weight_in, weight_out),
        8 * local_experts * rows * width * hidden,
    )
    back = exchange(parts)
    grad_in, grad_out = call(
        weights_kernel,
        (
            shape((local_experts, width, hidden), BF16),
            shape((local_experts, hidden, width), BF16),
        ),
        (slot_rows, act, d_pre),
        4 * local_experts * rows * width * hidden,
        grid=(local_experts,),
        in_specs=[
            pl.BlockSpec((2, 1, rows, width), lambda e: (0, e, 0, 0)),
            pl.BlockSpec((1, rows, hidden), lambda e: (e, 0, 0)),
            pl.BlockSpec((1, rows, hidden), lambda e: (e, 0, 0)),
        ],
        out_specs=[
            pl.BlockSpec((1, width, hidden), lambda e: (e, 0, 0)),
            pl.BlockSpec((1, hidden, width), lambda e: (e, 0, 0)),
        ],
    )
    token_grad, terms = call(
        functools.partial(images_kernel, dims),
        (
            shape((images, TOK, width), BF16),
            shape((n_expert, n_hidden, local_slots, width // n_hidden), F32),
        ),
        (
            logits,
            inputs,
            out_grads,
            router,
            back.reshape(n_expert, n_hidden, images, 2 * local_slots, width),
        ),
        10 * images * slots * TOK * width,
    )
    router_parts = exchange(terms.reshape(devices, local_slots, width // n_hidden))
    router_grad = jnp.sum(router_parts, axis=0).T
    return token_grad.reshape(images * TOK, width), router_grad, grad_in, grad_out


def solution(mesh):
    return jax.shard_map(
        functools.partial(per_device, mesh.shape["expert"], mesh.shape["hidden"]),
        mesh=mesh,
        in_specs=(
            P(BOTH, None),
            P(BOTH, None),
            P(),
            P("expert", None, "hidden"),
            P("expert", "hidden", None),
        ),
        out_specs=(
            P(BOTH, None),
            P("hidden", "expert"),
            P("expert", None, "hidden"),
            P("expert", "hidden", None),
        ),
        check_vma=False,
    )
```

```python
import functools

import jax
import jax.numpy as jnp
from jax import lax
from jax.experimental import pallas as pl
from jax.experimental.pallas import tpu as pltpu
from jax.sharding import PartitionSpec as P

SLOTS = 2
TOK = 196
BOTH = ("expert", "hidden")
F32, BF16 = jnp.float32, jnp.bfloat16
NN = (((1,), (0,)), ((), ()))
NT = (((1,), (1,)), ((), ()))
TN = (((0,), (0,)), ((), ()))


def dot(left, right, dims=NN):
    return lax.dot_general(left, right, dims, preferred_element_type=F32)


def reorder(shape, old_axes, rows):
    out_row = lax.broadcasted_iota(jnp.int32, (rows, 1), 0)
    strides = [1] * len(shape)
    for axis in reversed(range(len(shape) - 1)):
        strides[axis] = strides[axis + 1] * shape[axis + 1]
    source = jnp.zeros_like(out_row)
    rest = out_row
    for axis in reversed(old_axes):
        source = source + lax.rem(rest, shape[axis]) * strides[axis]
        rest = lax.div(rest, shape[axis])
    columns = lax.broadcasted_iota(jnp.int32, (rows, rows), 1)
    return jnp.where(columns == source, 1.0, 0.0).astype(BF16)


def softmaxes(logits):
    by_token = jnp.exp(logits - jnp.max(logits, axis=1, keepdims=True))
    dispatch = by_token / jnp.sum(by_token, axis=1, keepdims=True)
    by_slot = jnp.exp(logits - jnp.max(logits, axis=0, keepdims=True))
    combine = by_slot / jnp.sum(by_slot, axis=0, keepdims=True)
    return dispatch, combine


def slots_kernel(dims, tokens_hbm, out_grad_hbm, router_hbm, logits_out, sent, *scratch):
    tokens, out_grad, router, sems = scratch
    n_expert, n_hidden, local_slots = dims
    images, _, width = tokens.shape
    slots = n_expert * local_slots
    copies = [
        pltpu.make_async_copy(source, target, sems.at[i])
        for i, (source, target) in enumerate(
            ((router_hbm, router), (tokens_hbm, tokens), (out_grad_hbm, out_grad))
        )
    ]
    for copy in copies:
        copy.start()
    order = reorder((2, n_expert, local_slots), (1, 0, 2), 2 * slots)
    copies[0].wait()
    copies[1].wait()
    for image in range(images):
        logits = dot(router[...], tokens[image], NT)
        logits_out[image] = logits
        dispatch, combine = softmaxes(logits)
        slot_in = dot(dispatch.astype(BF16), tokens[image]).astype(BF16)
        if image == 0:
            copies[2].wait()
        slot_grad = dot(combine.astype(BF16), out_grad[image]).astype(BF16)
        both = dot(order, jnp.concatenate([slot_in, slot_grad], axis=0)).astype(BF16)
        both = both.reshape(n_expert, 2 * local_slots, width)
        for copy in range(n_hidden):
            sent[:, copy, image] = both


def experts_kernel(dims, received, weight_in, weight_out, parts, rows_out, act_out, d_pre_out):
    images, local_experts, chunk = dims
    devices, per_source, width = received.shape
    shape = (chunk, images, 2, local_experts, SLOTS)
    size = chunk * per_source
    part = size // (2 * local_experts)
    to_expert = (2, 3, 0, 1, 4)
    order = reorder(shape, to_expert, size)
    moved = tuple(shape[axis] for axis in to_expert)
    back = reorder(moved, tuple(to_expert.index(axis) for axis in range(5)), size)
    for start in range(0, devices, chunk):
        block = received[start : start + chunk].reshape(size, width)
        rows = dot(order, block).astype(BF16)
        base = start // chunk * part
        forwards, backwards = [], []
        for expert in range(local_experts):
            slot_in = rows[expert * part : (expert + 1) * part]
            slot_grad = rows[(local_experts + expert) * part : (local_experts + expert + 1) * part]
            rows_out[0, expert, base : base + part] = slot_in
            rows_out[1, expert, base : base + part] = slot_grad
            pre = dot(slot_in, weight_in[expert])
            d_act = dot(slot_grad, weight_out[expert], NT)
            half = 0.5 * (1.0 + lax.erf(pre * 0.7071067811865476))
            act = (pre * half).astype(BF16)
            slope = half + pre * jnp.exp(-0.5 * pre * pre) * 0.3989422804014327
            d_pre = (d_act * slope).astype(BF16)
            act_out[expert, base : base + part] = act
            d_pre_out[expert, base : base + part] = d_pre
            forwards.append(dot(act, weight_out[expert]).astype(BF16))
            backwards.append(dot(d_pre, weight_in[expert], NT).astype(BF16))
        results = dot(back, jnp.concatenate(forwards + backwards, axis=0)).astype(BF16)
        parts[start : start + chunk] = results.reshape(chunk, per_source, width)


def weights_kernel(rows, act, d_pre, grad_in, grad_out):
    grad_in[0] = dot(rows[0, 0], d_pre[0], TN).astype(BF16)
    grad_out[0] = dot(act[0], rows[1, 0], TN).astype(BF16)


def images_kernel(dims, logits_in, tokens, out_grad, router, parts, token_grad, terms):
    n_expert, n_hidden, local_slots = dims
    images, _, width = tokens.shape
    slots = n_expert * local_slots
    order = reorder((n_expert, 2, local_slots), (1, 0, 2), 2 * slots)
    total = None
    for image in range(images):
        dispatch, combine = softmaxes(logits_in[image])
        summed = parts[:, 0, image].astype(F32)
        for part in range(1, n_hidden):
            summed = summed + parts[:, part, image].astype(F32)
        summed = summed.reshape(2 * slots, width).astype(BF16)
        both = dot(order, summed).astype(BF16)
        slot_out, slot_in_grad = both[:slots], both[slots:]
        d_combine = dot(slot_out, out_grad[image], NT)
        d_dispatch = dot(slot_in_grad, tokens[image], NT)
        from_combine = combine * (d_combine - jnp.sum(combine * d_combine, axis=0, keepdims=True))
        from_dispatch = dispatch * (
            d_dispatch - jnp.sum(dispatch * d_dispatch, axis=1, keepdims=True)
        )
        d_logits = (from_combine + from_dispatch).astype(BF16)
        term = dot(d_logits, tokens[image])
        total = term if total is None else total + term
        left = jnp.concatenate([dispatch.astype(BF16), d_logits], axis=0)
        right = jnp.concatenate([slot_in_grad, router[...]], axis=0)
        token_grad[image] = dot(left, right, TN).astype(BF16)
    block = width // n_hidden
    for part in range(n_hidden):
        columns = total[:, part * block : (part + 1) * block]
        terms[:, part] = columns.reshape(n_expert, local_slots, block)


def exchange(blocks):
    return lax.all_to_all(blocks, BOTH, split_axis=0, concat_axis=0, tiled=True)


def call(kernel, outs, args, flops, **more):
    moved = sum(x.size * x.dtype.itemsize for x in list(outs) + list(args))
    return pl.pallas_call(
        kernel,
        out_shape=outs,
        cost_estimate=pl.CostEstimate(flops=flops, bytes_accessed=moved, transcendentals=0),
        compiler_params=pltpu.CompilerParams(vmem_limit_bytes=40 * 2**20),
        **more,
    )(*args)


def per_device(n_expert, n_hidden, tokens, out_grad, slot_router, weight_in, weight_out):
    width = tokens.shape[1]
    images = tokens.shape[0] // TOK
    local_experts, _, hidden = weight_in.shape
    local_slots = local_experts * SLOTS
    slots = n_expert * local_slots
    devices = n_expert * n_hidden
    per_source = 2 * images * local_slots
    rows = devices * images * SLOTS
    shape = jax.ShapeDtypeStruct
    inputs = tokens.reshape(images, TOK, width)
    out_grads = out_grad.reshape(images, TOK, width)
    router = slot_router.T
    dims = (n_expert, n_hidden, local_slots)

    logits, sent = call(
        functools.partial(slots_kernel, dims),
        (
            shape((images, slots, TOK), F32),
            shape((n_expert, n_hidden, images, 2 * local_slots, width), BF16),
        ),
        tuple(pltpu.with_memory_space_constraint(x, pltpu.HBM) for x in (inputs, out_grads, router)),
        8 * local_experts * rows * width * hidden * n_expert,
        in_specs=[pl.BlockSpec(memory_space=pltpu.HBM)] * 3,
        scratch_shapes=[
            pltpu.VMEM(inputs.shape, BF16),
            pltpu.VMEM(out_grads.shape, BF16),
            pltpu.VMEM(router.shape, BF16),
            pltpu.SemaphoreType.DMA((3,)),
        ],
    )
    received = exchange(sent.reshape(devices, per_source, width))
    chunk = max(c for c in range(1, devices + 1) if devices % c == 0 and c * per_source <= 256)
    parts, slot_rows, act, d_pre = call(
        functools.partial(experts_kernel, (images, local_experts, chunk)),
        (
            shape((devices, per_source, width), BF16),
            shape((2, local_experts, rows, width), BF16),
            shape((local_experts, rows, hidden), BF16),
            shape((local_experts, rows, hidden), BF16),
        ),
        (received, weight_in, weight_out),
        8 * local_experts * rows * width * hidden,
    )
    back = exchange(parts)
    grad_in, grad_out = call(
        weights_kernel,
        (
            shape((local_experts, width, hidden), BF16),
            shape((local_experts, hidden, width), BF16),
        ),
        (slot_rows, act, d_pre),
        4 * local_experts * rows * width * hidden,
        grid=(local_experts,),
        in_specs=[
            pl.BlockSpec((2, 1, rows, width), lambda e: (0, e, 0, 0)),
            pl.BlockSpec((1, rows, hidden), lambda e: (e, 0, 0)),
            pl.BlockSpec((1, rows, hidden), lambda e: (e, 0, 0)),
        ],
        out_specs=[
            pl.BlockSpec((1, width, hidden), lambda e: (e, 0, 0)),
            pl.BlockSpec((1, hidden, width), lambda e: (e, 0, 0)),
        ],
    )
    token_grad, terms = call(
        functools.partial(images_kernel, dims),
        (
            shape((images, TOK, width), BF16),
            shape((n_expert, n_hidden, local_slots, width // n_hidden), F32),
        ),
        (
            logits,
            inputs,
            out_grads,
            router,
            back.reshape(n_expert, n_hidden, images, 2 * local_slots, width),
        ),
        10 * images * slots * TOK * width,
    )
    router_parts = exchange(terms.reshape(devices, local_slots, width // n_hidden))
    router_grad = jnp.sum(router_parts, axis=0).T
    return token_grad.reshape(images * TOK, width), router_grad, grad_in, grad_out


def solution(mesh):
    return jax.shard_map(
        functools.partial(per_device, mesh.shape["expert"], mesh.shape["hidden"]),
        mesh=mesh,
        in_specs=(
            P(BOTH, None),
            P(BOTH, None),
            P(),
            P("expert", None, "hidden"),
            P("expert", "hidden", None),
        ),
        out_specs=(
            P(BOTH, None),
            P("hidden", "expert"),
            P("expert", None, "hidden"),
            P("expert", "hidden", None),
        ),
        check_vma=False,
    )
```

```python
import functools

import jax
import jax.numpy as jnp
from jax import lax
from jax.experimental import pallas as pl
from jax.experimental.pallas import tpu as pltpu
from jax.sharding import PartitionSpec as P

SLOTS = 2
TOK = 196
BOTH = ("expert", "hidden")
F32, BF16 = jnp.float32, jnp.bfloat16
NN = (((1,), (0,)), ((), ()))
NT = (((1,), (1,)), ((), ()))
TN = (((0,), (0,)), ((), ()))


def dot(left, right, dims=NN):
    return lax.dot_general(left, right, dims, preferred_element_type=F32)


def reorder(shape, old_axes, rows):
    out_row = lax.broadcasted_iota(jnp.int32, (rows, 1), 0)
    strides = [1] * len(shape)
    for axis in reversed(range(len(shape) - 1)):
        strides[axis] = strides[axis + 1] * shape[axis + 1]
    source = jnp.zeros_like(out_row)
    rest = out_row
    for axis in reversed(old_axes):
        source = source + lax.rem(rest, shape[axis]) * strides[axis]
        rest = lax.div(rest, shape[axis])
    columns = lax.broadcasted_iota(jnp.int32, (rows, rows), 1)
    return jnp.where(columns == source, 1.0, 0.0).astype(BF16)


def softmaxes(logits):
    by_token = jnp.exp(logits - jnp.max(logits, axis=1, keepdims=True))
    dispatch = by_token / jnp.sum(by_token, axis=1, keepdims=True)
    by_slot = jnp.exp(logits - jnp.max(logits, axis=0, keepdims=True))
    combine = by_slot / jnp.sum(by_slot, axis=0, keepdims=True)
    return dispatch, combine


def slots_kernel(dims, tokens_hbm, out_grad_hbm, router_hbm, logits_out, sent, *scratch):
    tokens, out_grad, router, sems = scratch
    n_expert, n_hidden, local_slots = dims
    images, _, width = tokens.shape
    slots = n_expert * local_slots
    copies = [
        pltpu.make_async_copy(source, target, sems.at[i])
        for i, (source, target) in enumerate(
            ((router_hbm, router), (tokens_hbm, tokens), (out_grad_hbm, out_grad))
        )
    ]
    for copy in copies:
        copy.start()
    order = reorder((2, n_expert, local_slots), (1, 0, 2), 2 * slots)
    copies[0].wait()
    copies[1].wait()
    for image in range(images):
        logits = dot(router[...], tokens[image], NT)
        logits_out[image] = logits
        dispatch, combine = softmaxes(logits)
        slot_in = dot(dispatch.astype(BF16), tokens[image]).astype(BF16)
        if image == 0:
            copies[2].wait()
        slot_grad = dot(combine.astype(BF16), out_grad[image]).astype(BF16)
        both = dot(order, jnp.concatenate([slot_in, slot_grad], axis=0)).astype(BF16)
        both = both.reshape(n_expert, 2 * local_slots, width)
        for copy in range(n_hidden):
            sent[:, copy, image] = both


def experts_kernel(dims, received, weight_in, weight_out, parts, rows_out, act_out, d_pre_out, turned_in, turned_out):
    images, local_experts, chunk = dims
    devices, per_source, width = received.shape
    shape = (chunk, images, 2, local_experts, SLOTS)
    size = chunk * per_source
    part = size // (2 * local_experts)
    to_expert = (2, 3, 0, 1, 4)
    order = reorder(shape, to_expert, size)
    for e in range(local_experts):
        turned_out[e] = weight_out[e].T
        turned_in[e] = weight_in[e].T
    moved = tuple(shape[axis] for axis in to_expert)
    back = reorder(moved, tuple(to_expert.index(axis) for axis in range(5)), size)
    for start in range(0, devices, chunk):
        block = received[start : start + chunk].reshape(size, width)
        rows = dot(order, block).astype(BF16)
        base = start // chunk * part
        forwards, backwards = [], []
        for expert in range(local_experts):
            slot_in = rows[expert * part : (expert + 1) * part]
            slot_grad = rows[(local_experts + expert) * part : (local_experts + expert + 1) * part]
            rows_out[0, expert, base : base + part] = slot_in
            rows_out[1, expert, base : base + part] = slot_grad
            pre = dot(slot_in, weight_in[expert])
            d_act = dot(slot_grad, turned_out[expert])
            half = 0.5 * (1.0 + lax.erf(pre * 0.7071067811865476))
            act = (pre * half).astype(BF16)
            slope = half + pre * jnp.exp(-0.5 * pre * pre) * 0.3989422804014327
            d_pre = (d_act * slope).astype(BF16)
            act_out[expert, base : base + part] = act
            d_pre_out[expert, base : base + part] = d_pre
            forwards.append(dot(act, weight_out[expert]).astype(BF16))
            backwards.append(dot(d_pre, turned_in[expert]).astype(BF16))
        results = dot(back, jnp.concatenate(forwards + backwards, axis=0)).astype(BF16)
        parts[start : start + chunk] = results.reshape(chunk, per_source, width)


def weights_kernel(rows, act, d_pre, grad_in, grad_out):
    grad_in[0] = dot(rows[0, 0], d_pre[0], TN).astype(BF16)
    grad_out[0] = dot(act[0], rows[1, 0], TN).astype(BF16)


def images_kernel(dims, logits_in, tokens, out_grad, parts, terms, left_out, right_out):
    n_expert, n_hidden, local_slots = dims
    images, _, width = tokens.shape
    slots = n_expert * local_slots
    order = reorder((n_expert, 2, local_slots), (1, 0, 2), 2 * slots)
    total = None
    for image in range(images):
        dispatch, combine = softmaxes(logits_in[image])
        summed = parts[:, 0, image].astype(F32)
        for part in range(1, n_hidden):
            summed = summed + parts[:, part, image].astype(F32)
        summed = summed.reshape(2 * slots, width).astype(BF16)
        both = dot(order, summed).astype(BF16)
        slot_out, slot_in_grad = both[:slots], both[slots:]
        d_combine = dot(slot_out, out_grad[image], NT)
        d_dispatch = dot(slot_in_grad, tokens[image], NT)
        from_combine = combine * (d_combine - jnp.sum(combine * d_combine, axis=0, keepdims=True))
        from_dispatch = dispatch * (
            d_dispatch - jnp.sum(dispatch * d_dispatch, axis=1, keepdims=True)
        )
        d_logits = (from_combine + from_dispatch).astype(BF16)
        term = dot(d_logits, tokens[image])
        total = term if total is None else total + term
        left_out[image, :slots] = dispatch.astype(BF16)
        left_out[image, slots:] = d_logits
        right_out[image] = slot_in_grad
    block = width // n_hidden
    for part in range(n_hidden):
        columns = total[:, part * block : (part + 1) * block]
        terms[:, part] = columns.reshape(n_expert, local_slots, block).astype(BF16)


def tokens_kernel(left, slot_in_grad, router, token_grad):
    for image in range(left.shape[0]):
        right = jnp.concatenate([slot_in_grad[image], router[...]], axis=0)
        token_grad[image] = dot(left[image], right, TN).astype(BF16)


def exchange(blocks):
    return lax.all_to_all(blocks, BOTH, split_axis=0, concat_axis=0, tiled=True)


def call(kernel, outs, args, flops, **more):
    moved = sum(x.size * x.dtype.itemsize for x in list(outs) + list(args))
    return pl.pallas_call(
        kernel,
        out_shape=outs,
        cost_estimate=pl.CostEstimate(flops=flops, bytes_accessed=moved, transcendentals=0),
        compiler_params=pltpu.CompilerParams(vmem_limit_bytes=40 * 2**20),
        **more,
    )(*args)


def per_device(n_expert, n_hidden, tokens, out_grad, slot_router, weight_in, weight_out):
    width = tokens.shape[1]
    images = tokens.shape[0] // TOK
    local_experts, _, hidden = weight_in.shape
    local_slots = local_experts * SLOTS
    slots = n_expert * local_slots
    devices = n_expert * n_hidden
    per_source = 2 * images * local_slots
    rows = devices * images * SLOTS
    shape = jax.ShapeDtypeStruct
    inputs = tokens.reshape(images, TOK, width)
    out_grads = out_grad.reshape(images, TOK, width)
    router = slot_router.T
    dims = (n_expert, n_hidden, local_slots)

    logits, sent = call(
        functools.partial(slots_kernel, dims),
        (
            shape((images, slots, TOK), F32),
            shape((n_expert, n_hidden, images, 2 * local_slots, width), BF16),
        ),
        tuple(pltpu.with_memory_space_constraint(x, pltpu.HBM) for x in (inputs, out_grads, router)),
        8 * local_experts * rows * width * hidden * n_expert,
        in_specs=[pl.BlockSpec(memory_space=pltpu.HBM)] * 3,
        scratch_shapes=[
            pltpu.VMEM(inputs.shape, BF16),
            pltpu.VMEM(out_grads.shape, BF16),
            pltpu.VMEM(router.shape, BF16),
            pltpu.SemaphoreType.DMA((3,)),
        ],
    )
    received = exchange(sent.reshape(devices, per_source, width))
    chunk = max(c for c in range(1, devices + 1) if devices % c == 0 and c * per_source <= 256)
    parts, slot_rows, act, d_pre = call(
        functools.partial(experts_kernel, (images, local_experts, chunk)),
        (
            shape((devices, per_source, width), BF16),
            shape((2, local_experts, rows, width), BF16),
            shape((local_experts, rows, hidden), BF16),
            shape((local_experts, rows, hidden), BF16),
        ),
        (received, weight_in, weight_out),
        8 * local_experts * rows * width * hidden,
        scratch_shapes=[pltpu.VMEM((local_experts, hidden, width), BF16), pltpu.VMEM((local_experts, width, hidden), BF16)],
    )
    back = exchange(parts)
    grad_in, grad_out = call(
        weights_kernel,
        (
            shape((local_experts, width, hidden), BF16),
            shape((local_experts, hidden, width), BF16),
        ),
        (slot_rows, act, d_pre),
        4 * local_experts * rows * width * hidden,
        grid=(local_experts,),
        in_specs=[
            pl.BlockSpec((2, 1, rows, width), lambda e: (0, e, 0, 0)),
            pl.BlockSpec((1, rows, hidden), lambda e: (e, 0, 0)),
            pl.BlockSpec((1, rows, hidden), lambda e: (e, 0, 0)),
        ],
        out_specs=[
            pl.BlockSpec((1, width, hidden), lambda e: (e, 0, 0)),
            pl.BlockSpec((1, hidden, width), lambda e: (e, 0, 0)),
        ],
    )
    terms, left, slot_in_grad = call(
        functools.partial(images_kernel, dims),
        (
            shape((n_expert, n_hidden, local_slots, width // n_hidden), BF16),
            shape((images, 2 * slots, TOK), BF16),
            shape((images, slots, width), BF16),
        ),
        (
            logits,
            inputs,
            out_grads,
            back.reshape(n_expert, n_hidden, images, 2 * local_slots, width),
        ),
        6 * images * slots * TOK * width,
    )
    (token_grad,) = call(
        tokens_kernel,
        (shape((images, TOK, width), BF16),),
        (left, slot_in_grad, router),
        4 * images * slots * TOK * width,
    )
    router_parts = exchange(terms.reshape(devices, local_slots, width // n_hidden))
    router_grad = jnp.sum(router_parts.astype(F32), axis=0).T
    return token_grad.reshape(images * TOK, width), router_grad, grad_in, grad_out


def solution(mesh):
    return jax.shard_map(
        functools.partial(per_device, mesh.shape["expert"], mesh.shape["hidden"]),
        mesh=mesh,
        in_specs=(
            P(BOTH, None),
            P(BOTH, None),
            P(),
            P("expert", None, "hidden"),
            P("expert", "hidden", None),
        ),
        out_specs=(
            P(BOTH, None),
            P("hidden", "expert"),
            P("expert", None, "hidden"),
            P("expert", "hidden", None),
        ),
        check_vma=False,
    )
```

```python
import functools

import jax
import jax.numpy as jnp
from jax import lax
from jax.experimental import pallas as pl
from jax.experimental.pallas import tpu as pltpu
from jax.sharding import PartitionSpec as P

SLOTS = 2
TOK = 196
BOTH = ("expert", "hidden")
F32, BF16 = jnp.float32, jnp.bfloat16
NN = (((1,), (0,)), ((), ()))
NT = (((1,), (1,)), ((), ()))
TN = (((0,), (0,)), ((), ()))


def dot(left, right, dims=NN):
    return lax.dot_general(left, right, dims, preferred_element_type=F32)


def reorder(shape, old_axes, rows):
    out_row = lax.broadcasted_iota(jnp.int32, (rows, 1), 0)
    strides = [1] * len(shape)
    for axis in reversed(range(len(shape) - 1)):
        strides[axis] = strides[axis + 1] * shape[axis + 1]
    source = jnp.zeros_like(out_row)
    rest = out_row
    for axis in reversed(old_axes):
        source = source + lax.rem(rest, shape[axis]) * strides[axis]
        rest = lax.div(rest, shape[axis])
    columns = lax.broadcasted_iota(jnp.int32, (rows, rows), 1)
    return jnp.where(columns == source, 1.0, 0.0).astype(BF16)


def softmaxes(logits):
    by_token = jnp.exp(logits - jnp.max(logits, axis=1, keepdims=True))
    dispatch = by_token / jnp.sum(by_token, axis=1, keepdims=True)
    by_slot = jnp.exp(logits - jnp.max(logits, axis=0, keepdims=True))
    combine = by_slot / jnp.sum(by_slot, axis=0, keepdims=True)
    return dispatch, combine


def slots_kernel(dims, tokens_hbm, out_grad_hbm, router_hbm, logits_out, sent, *scratch):
    tokens, out_grad, router, sems = scratch
    n_expert, n_hidden, local_slots = dims
    images, _, width = tokens.shape
    slots = n_expert * local_slots
    copies = [
        pltpu.make_async_copy(source, target, sems.at[i])
        for i, (source, target) in enumerate(
            ((tokens_hbm, tokens), (router_hbm, router), (out_grad_hbm, out_grad))
        )
    ]
    for copy in copies:
        copy.start()
    copies[0].wait()
    copies[1].wait()
    for image in range(images):
        logits = dot(router[...], tokens[image].T)
        logits_out[image] = logits
        dispatch, combine = softmaxes(logits)
        slot_in = dot(dispatch.astype(BF16), tokens[image]).astype(BF16)
        if image == 0:
            copies[2].wait()
        slot_grad = dot(combine.astype(BF16), out_grad[image]).astype(BF16)
        for expert in range(n_expert):
            own = slice(expert * local_slots, (expert + 1) * local_slots)
            block = jnp.concatenate([slot_in[own], slot_grad[own]], axis=0)
            for copy in range(n_hidden):
                sent[expert, copy, image] = block


def experts_kernel(dims, received, weight_in, weight_out, parts, rows_out, act_out, d_pre_out, turned_in, turned_out):
    images, local_experts, chunk = dims
    devices, per_source, width = received.shape
    shape = (chunk, images, 2, local_experts, SLOTS)
    size = chunk * per_source
    part = size // (2 * local_experts)
    to_expert = (2, 3, 0, 1, 4)
    order = reorder(shape, to_expert, size)
    for e in range(local_experts):
        turned_out[e] = weight_out[e].T
        turned_in[e] = weight_in[e].T
    moved = tuple(shape[axis] for axis in to_expert)
    back = reorder(moved, tuple(to_expert.index(axis) for axis in range(5)), size)
    for start in range(0, devices, chunk):
        block = received[start : start + chunk].reshape(size, width)
        rows = dot(order, block).astype(BF16)
        base = start // chunk * part
        forwards, backwards = [], []
        for expert in range(local_experts):
            slot_in = rows[expert * part : (expert + 1) * part]
            slot_grad = rows[(local_experts + expert) * part : (local_experts + expert + 1) * part]
            rows_out[0, expert, base : base + part] = slot_in
            rows_out[1, expert, base : base + part] = slot_grad
            pre = dot(slot_in, weight_in[expert])
            d_act = dot(slot_grad, turned_out[expert])
            half = 0.5 * (1.0 + lax.erf(pre * 0.7071067811865476))
            act = (pre * half).astype(BF16)
            slope = half + pre * jnp.exp(-0.5 * pre * pre) * 0.3989422804014327
            d_pre = (d_act * slope).astype(BF16)
            act_out[expert, base : base + part] = act
            d_pre_out[expert, base : base + part] = d_pre
            forwards.append(dot(act, weight_out[expert]).astype(BF16))
            backwards.append(dot(d_pre, turned_in[expert]).astype(BF16))
        results = dot(back, jnp.concatenate(forwards + backwards, axis=0)).astype(BF16)
        parts[start : start + chunk] = results.reshape(chunk, per_source, width)


def weights_kernel(rows, act, d_pre, grad_in, grad_out):
    grad_in[0] = dot(rows[0, 0], d_pre[0], TN).astype(BF16)
    grad_out[0] = dot(act[0], rows[1, 0], TN).astype(BF16)


def images_kernel(dims, logits_in, tokens, out_grad, parts, terms, left_out, right_out):
    n_expert, n_hidden, local_slots = dims
    images, _, width = tokens.shape
    slots = n_expert * local_slots
    block = width // n_hidden
    totals = [jnp.zeros((slots, block), F32)] * n_hidden
    for image in range(images):
        dispatch, combine = softmaxes(logits_in[image])
        summed = parts[:, 0, image].astype(F32)
        for part in range(1, n_hidden):
            summed = summed + parts[:, part, image].astype(F32)
        slot_out = summed[:, :local_slots].reshape(slots, width).astype(BF16)
        slot_in_grad = summed[:, local_slots:].reshape(slots, width).astype(BF16)
        d_combine = dot(slot_out, out_grad[image].T)
        d_dispatch = dot(slot_in_grad, tokens[image].T)
        from_combine = combine * (d_combine - jnp.sum(combine * d_combine, axis=0, keepdims=True))
        from_dispatch = dispatch * (
            d_dispatch - jnp.sum(dispatch * d_dispatch, axis=1, keepdims=True)
        )
        d_logits = (from_combine + from_dispatch).astype(BF16)
        for part in range(n_hidden):
            columns = tokens[image, :, part * block : (part + 1) * block]
            totals[part] = totals[part] + dot(d_logits, columns)
        left_out[image, :slots] = dispatch.astype(BF16)
        left_out[image, slots:] = d_logits
        right_out[image] = slot_in_grad
    for part in range(n_hidden):
        terms[:, part] = totals[part].reshape(n_expert, local_slots, block).astype(BF16)


def tokens_kernel(left, slot_in_grad, router, token_grad):
    for image in range(left.shape[0]):
        right = jnp.concatenate([slot_in_grad[image], router[...]], axis=0)
        token_grad[image] = dot(left[image], right, TN).astype(BF16)


def exchange(blocks):
    return lax.all_to_all(blocks, BOTH, split_axis=0, concat_axis=0, tiled=True)


def call(kernel, outs, args, flops, **more):
    moved = sum(x.size * x.dtype.itemsize for x in list(outs) + list(args))
    return pl.pallas_call(
        kernel,
        out_shape=outs,
        cost_estimate=pl.CostEstimate(flops=flops, bytes_accessed=moved, transcendentals=0),
        compiler_params=pltpu.CompilerParams(vmem_limit_bytes=40 * 2**20),
        **more,
    )(*args)


def per_device(n_expert, n_hidden, tokens, out_grad, slot_router, weight_in, weight_out):
    width = tokens.shape[1]
    images = tokens.shape[0] // TOK
    local_experts, _, hidden = weight_in.shape
    local_slots = local_experts * SLOTS
    slots = n_expert * local_slots
    devices = n_expert * n_hidden
    per_source = 2 * images * local_slots
    rows = devices * images * SLOTS
    shape = jax.ShapeDtypeStruct
    inputs = tokens.reshape(images, TOK, width)
    out_grads = out_grad.reshape(images, TOK, width)
    router = slot_router.T
    dims = (n_expert, n_hidden, local_slots)

    logits, sent = call(
        functools.partial(slots_kernel, dims),
        (
            shape((images, slots, TOK), F32),
            shape((n_expert, n_hidden, images, 2 * local_slots, width), BF16),
        ),
        tuple(pltpu.with_memory_space_constraint(x, pltpu.HBM) for x in (inputs, out_grads, router)),
        6 * images * slots * TOK * width,
        in_specs=[pl.BlockSpec(memory_space=pltpu.HBM)] * 3,
        scratch_shapes=[
            pltpu.VMEM(inputs.shape, BF16),
            pltpu.VMEM(out_grads.shape, BF16),
            pltpu.VMEM(router.shape, BF16),
            pltpu.SemaphoreType.DMA((3,)),
        ],
    )
    (sent,) = call(
        lambda given, kept: None,
        (shape(sent.shape, BF16),),
        (sent,),
        8 * local_experts * rows * width * hidden * n_expert,
        in_specs=[pl.BlockSpec(memory_space=pl.ANY)],
        out_specs=[pl.BlockSpec(memory_space=pl.ANY)],
        input_output_aliases={0: 0},
    )
    received = exchange(sent.reshape(devices, per_source, width))
    chunk = max(c for c in range(1, devices + 1) if devices % c == 0 and c * per_source <= 256)
    parts, slot_rows, act, d_pre = call(
        functools.partial(experts_kernel, (images, local_experts, chunk)),
        (
            shape((devices, per_source, width), BF16),
            shape((2, local_experts, rows, width), BF16),
            shape((local_experts, rows, hidden), BF16),
            shape((local_experts, rows, hidden), BF16),
        ),
        (received, weight_in, weight_out),
        8 * local_experts * rows * width * hidden,
        scratch_shapes=[pltpu.VMEM((local_experts, hidden, width), BF16), pltpu.VMEM((local_experts, width, hidden), BF16)],
    )
    back = exchange(parts)
    grad_in, grad_out = call(
        weights_kernel,
        (
            shape((local_experts, width, hidden), BF16),
            shape((local_experts, hidden, width), BF16),
        ),
        (slot_rows, act, d_pre),
        4 * local_experts * rows * width * hidden,
        grid=(local_experts,),
        in_specs=[
            pl.BlockSpec((2, 1, rows, width), lambda e: (0, e, 0, 0)),
            pl.BlockSpec((1, rows, hidden), lambda e: (e, 0, 0)),
            pl.BlockSpec((1, rows, hidden), lambda e: (e, 0, 0)),
        ],
        out_specs=[
            pl.BlockSpec((1, width, hidden), lambda e: (e, 0, 0)),
            pl.BlockSpec((1, hidden, width), lambda e: (e, 0, 0)),
        ],
    )
    terms, left, slot_in_grad = call(
        functools.partial(images_kernel, dims),
        (
            shape((n_expert, n_hidden, local_slots, width // n_hidden), BF16),
            shape((images, 2 * slots, TOK), BF16),
            shape((images, slots, width), BF16),
        ),
        (
            logits,
            inputs,
            out_grads,
            back.reshape(n_expert, n_hidden, images, 2 * local_slots, width),
        ),
        6 * images * slots * TOK * width,
    )
    (token_grad,) = call(
        tokens_kernel,
        (shape((images, TOK, width), BF16),),
        (left, slot_in_grad, router),
        4 * images * slots * TOK * width,
    )
    router_parts = exchange(terms.reshape(devices, local_slots, width // n_hidden))
    router_grad = jnp.sum(router_parts.astype(F32), axis=0).T
    return token_grad.reshape(images * TOK, width), router_grad, grad_in, grad_out


def solution(mesh):
    return jax.shard_map(
        functools.partial(per_device, mesh.shape["expert"], mesh.shape["hidden"]),
        mesh=mesh,
        in_specs=(
            P(BOTH, None),
            P(BOTH, None),
            P(),
            P("expert", None, "hidden"),
            P("expert", "hidden", None),
        ),
        out_specs=(
            P(BOTH, None),
            P("hidden", "expert"),
            P("expert", None, "hidden"),
            P("expert", "hidden", None),
        ),
        check_vma=False,
    )
```

```python
import functools
import math

import jax
import jax.numpy as jnp
from jax import lax
from jax.experimental import pallas as pl
from jax.experimental.pallas import tpu as pltpu
from jax.sharding import PartitionSpec as P

SLOTS = 2
TOK = 196
BOTH = ("expert", "hidden")
STRIDES = (19, 3, 15)
F32, BF16 = jnp.float32, jnp.bfloat16
NN = (((1,), (0,)), ((), ()))
NT = (((1,), (1,)), ((), ()))
TN = (((0,), (0,)), ((), ()))


def dot(left, right, dims=NN):
    return lax.dot_general(left, right, dims, preferred_element_type=F32)


def reorder(shape, old_axes, rows):
    out_row = lax.broadcasted_iota(jnp.int32, (rows, 1), 0)
    strides = [1] * len(shape)
    for axis in reversed(range(len(shape) - 1)):
        strides[axis] = strides[axis + 1] * shape[axis + 1]
    source = jnp.zeros_like(out_row)
    rest = out_row
    for axis in reversed(old_axes):
        source = source + lax.rem(rest, shape[axis]) * strides[axis]
        rest = lax.div(rest, shape[axis])
    columns = lax.broadcasted_iota(jnp.int32, (rows, rows), 1)
    return jnp.where(columns == source, 1.0, 0.0).astype(BF16)


def ring(devices, stride):
    if math.gcd(devices, stride) != 1:
        stride = 1
    return [stride * place % devices for place in range(devices)]


def places(devices, stride):
    return {device: place for place, device in enumerate(ring(devices, stride))}


def softmaxes(logits):
    by_token = jnp.exp(logits - jnp.max(logits, axis=1, keepdims=True))
    dispatch = by_token / jnp.sum(by_token, axis=1, keepdims=True)
    by_slot = jnp.exp(logits - jnp.max(logits, axis=0, keepdims=True))
    combine = by_slot / jnp.sum(by_slot, axis=0, keepdims=True)
    return dispatch, combine


def slots_kernel(dims, tokens_hbm, out_grad_hbm, router_hbm, logits_out, sent, *scratch):
    tokens, out_grad, router, sems = scratch
    n_expert, n_hidden, local_slots = dims
    images, _, width = tokens.shape
    place = places(n_expert * n_hidden, STRIDES[0])
    copies = [
        pltpu.make_async_copy(source, target, sems.at[i])
        for i, (source, target) in enumerate(
            ((tokens_hbm, tokens), (router_hbm, router), (out_grad_hbm, out_grad))
        )
    ]
    for copy in copies:
        copy.start()
    copies[0].wait()
    copies[1].wait()
    for image in range(images):
        logits = dot(router[...], tokens[image].T)
        logits_out[image] = logits
        dispatch, combine = softmaxes(logits)
        slot_in = dot(dispatch.astype(BF16), tokens[image]).astype(BF16)
        if image == 0:
            copies[2].wait()
        slot_grad = dot(combine.astype(BF16), out_grad[image]).astype(BF16)
        for expert in range(n_expert):
            own = slice(expert * local_slots, (expert + 1) * local_slots)
            block = jnp.concatenate([slot_in[own], slot_grad[own]], axis=0)
            for part in range(n_hidden):
                sent[place[expert * n_hidden + part], image] = block


def experts_kernel(dims, received, weight_in, weight_out, parts, rows_out, act_out, d_pre_out, turned_in, turned_out):
    images, local_experts, chunk = dims
    devices, per_source, width = received.shape
    source, place = ring(devices, STRIDES[0]), places(devices, STRIDES[1])
    shape = (chunk, images, 2, local_experts, SLOTS)
    size = chunk * per_source
    part = size // (2 * local_experts)
    to_expert = (2, 3, 0, 1, 4)
    order = reorder(shape, to_expert, size)
    for e in range(local_experts):
        turned_out[e] = weight_out[e].T
        turned_in[e] = weight_in[e].T
    moved = tuple(shape[axis] for axis in to_expert)
    back = reorder(moved, tuple(to_expert.index(axis) for axis in range(5)), size)
    for start in range(0, devices, chunk):
        block = received[start : start + chunk].reshape(size, width)
        rows = dot(order, block).astype(BF16)
        base = start // chunk * part
        forwards, backwards = [], []
        for expert in range(local_experts):
            slot_in = rows[expert * part : (expert + 1) * part]
            slot_grad = rows[(local_experts + expert) * part : (local_experts + expert + 1) * part]
            rows_out[0, expert, base : base + part] = slot_in
            rows_out[1, expert, base : base + part] = slot_grad
            pre = dot(slot_in, weight_in[expert])
            d_act = dot(slot_grad, turned_out[expert])
            half = 0.5 * (1.0 + lax.erf(pre * 0.7071067811865476))
            act = (pre * half).astype(BF16)
            slope = half + pre * jnp.exp(-0.5 * pre * pre) * 0.3989422804014327
            d_pre = (d_act * slope).astype(BF16)
            act_out[expert, base : base + part] = act
            d_pre_out[expert, base : base + part] = d_pre
            forwards.append(dot(act, weight_out[expert]).astype(BF16))
            backwards.append(dot(d_pre, turned_in[expert]).astype(BF16))
        results = dot(back, jnp.concatenate(forwards + backwards, axis=0)).astype(BF16)
        results = results.reshape(chunk, per_source, width)
        for row in range(chunk):
            parts[place[source[start + row]]] = results[row]


def weights_kernel(rows, act, d_pre, grad_in, grad_out):
    grad_in[0] = dot(rows[0, 0], d_pre[0], TN).astype(BF16)
    grad_out[0] = dot(act[0], rows[1, 0], TN).astype(BF16)


def images_kernel(dims, logits_in, tokens, out_grad, parts, terms, left_out, right_out):
    n_expert, n_hidden, local_slots = dims
    images, _, width = tokens.shape
    slots = n_expert * local_slots
    place = places(n_expert * n_hidden, STRIDES[1])
    block = width // n_hidden
    totals = [jnp.zeros((slots, block), F32)] * n_hidden
    for image in range(images):
        dispatch, combine = softmaxes(logits_in[image])
        summed = []
        for expert in range(n_expert):
            held = [parts[place[expert * n_hidden + part], image] for part in range(n_hidden)]
            summed.append(sum(piece.astype(F32) for piece in held))
        summed = jnp.stack(summed)
        slot_out = summed[:, :local_slots].reshape(slots, width).astype(BF16)
        slot_in_grad = summed[:, local_slots:].reshape(slots, width).astype(BF16)
        d_combine = dot(slot_out, out_grad[image].T)
        d_dispatch = dot(slot_in_grad, tokens[image].T)
        from_combine = combine * (d_combine - jnp.sum(combine * d_combine, axis=0, keepdims=True))
        from_dispatch = dispatch * (
            d_dispatch - jnp.sum(dispatch * d_dispatch, axis=1, keepdims=True)
        )
        d_logits = (from_combine + from_dispatch).astype(BF16)
        for part in range(n_hidden):
            columns = tokens[image, :, part * block : (part + 1) * block]
            totals[part] = totals[part] + dot(d_logits, columns)
        left_out[image, :slots] = dispatch.astype(BF16)
        left_out[image, slots:] = d_logits
        right_out[image] = slot_in_grad
    place = places(n_expert * n_hidden, STRIDES[2])
    for part in range(n_hidden):
        for expert in range(n_expert):
            own = slice(expert * local_slots, (expert + 1) * local_slots)
            terms[place[expert * n_hidden + part]] = totals[part][own].astype(BF16)


def tokens_kernel(left, slot_in_grad, router, token_grad):
    for image in range(left.shape[0]):
        right = jnp.concatenate([slot_in_grad[image], router[...]], axis=0)
        token_grad[image] = dot(left[image], right, TN).astype(BF16)


def exchange(blocks, stride):
    order = [ring(blocks.shape[0], stride)]
    return lax.all_to_all(
        blocks, BOTH, split_axis=0, concat_axis=0, tiled=True, axis_index_groups=order
    )


def call(kernel, outs, args, flops, **more):
    moved = sum(x.size * x.dtype.itemsize for x in list(outs) + list(args))
    return pl.pallas_call(
        kernel,
        out_shape=outs,
        cost_estimate=pl.CostEstimate(flops=flops, bytes_accessed=moved, transcendentals=0),
        compiler_params=pltpu.CompilerParams(vmem_limit_bytes=40 * 2**20),
        **more,
    )(*args)


def per_device(n_expert, n_hidden, tokens, out_grad, slot_router, weight_in, weight_out):
    width = tokens.shape[1]
    images = tokens.shape[0] // TOK
    local_experts, _, hidden = weight_in.shape
    local_slots = local_experts * SLOTS
    slots = n_expert * local_slots
    devices = n_expert * n_hidden
    per_source = 2 * images * local_slots
    rows = devices * images * SLOTS
    shape = jax.ShapeDtypeStruct
    inputs = tokens.reshape(images, TOK, width)
    out_grads = out_grad.reshape(images, TOK, width)
    router = slot_router.T
    dims = (n_expert, n_hidden, local_slots)

    logits, sent = call(
        functools.partial(slots_kernel, dims),
        (
            shape((images, slots, TOK), F32),
            shape((devices, images, 2 * local_slots, width), BF16),
        ),
        tuple(pltpu.with_memory_space_constraint(x, pltpu.HBM) for x in (inputs, out_grads, router)),
        6 * images * slots * TOK * width,
        in_specs=[pl.BlockSpec(memory_space=pltpu.HBM)] * 3,
        scratch_shapes=[
            pltpu.VMEM(inputs.shape, BF16),
            pltpu.VMEM(out_grads.shape, BF16),
            pltpu.VMEM(router.shape, BF16),
            pltpu.SemaphoreType.DMA((3,)),
        ],
    )
    (sent,) = call(
        lambda given, kept: None,
        (shape(sent.shape, BF16),),
        (sent,),
        8 * local_experts * rows * width * hidden * n_expert,
        in_specs=[pl.BlockSpec(memory_space=pl.ANY)],
        out_specs=[pl.BlockSpec(memory_space=pl.ANY)],
        input_output_aliases={0: 0},
    )
    received = exchange(sent.reshape(devices, per_source, width), STRIDES[0])
    chunk = max(c for c in range(1, devices + 1) if devices % c == 0 and c * per_source <= 256)
    parts, slot_rows, act, d_pre = call(
        functools.partial(experts_kernel, (images, local_experts, chunk)),
        (
            shape((devices, per_source, width), BF16),
            shape((2, local_experts, rows, width), BF16),
            shape((local_experts, rows, hidden), BF16),
            shape((local_experts, rows, hidden), BF16),
        ),
        (received, weight_in, weight_out),
        8 * local_experts * rows * width * hidden,
        scratch_shapes=[pltpu.VMEM((local_experts, hidden, width), BF16), pltpu.VMEM((local_experts, width, hidden), BF16)],
    )
    back = exchange(parts, STRIDES[1])
    grad_in, grad_out = call(
        weights_kernel,
        (
            shape((local_experts, width, hidden), BF16),
            shape((local_experts, hidden, width), BF16),
        ),
        (slot_rows, act, d_pre),
        4 * local_experts * rows * width * hidden,
        grid=(local_experts,),
        in_specs=[
            pl.BlockSpec((2, 1, rows, width), lambda e: (0, e, 0, 0)),
            pl.BlockSpec((1, rows, hidden), lambda e: (e, 0, 0)),
            pl.BlockSpec((1, rows, hidden), lambda e: (e, 0, 0)),
        ],
        out_specs=[
            pl.BlockSpec((1, width, hidden), lambda e: (e, 0, 0)),
            pl.BlockSpec((1, hidden, width), lambda e: (e, 0, 0)),
        ],
    )
    terms, left, slot_in_grad = call(
        functools.partial(images_kernel, dims),
        (
            shape((devices, local_slots, width // n_hidden), BF16),
            shape((images, 2 * slots, TOK), BF16),
            shape((images, slots, width), BF16),
        ),
        (
            logits,
            inputs,
            out_grads,
            back.reshape(devices, images, 2 * local_slots, width),
        ),
        6 * images * slots * TOK * width,
    )
    (token_grad,) = call(
        tokens_kernel,
        (shape((images, TOK, width), BF16),),
        (left, slot_in_grad, router),
        4 * images * slots * TOK * width,
    )
    router_parts = exchange(terms, STRIDES[2])
    router_grad = jnp.sum(router_parts.astype(F32), axis=0).T
    return token_grad.reshape(images * TOK, width), router_grad, grad_in, grad_out


def solution(mesh):
    return jax.shard_map(
        functools.partial(per_device, mesh.shape["expert"], mesh.shape["hidden"]),
        mesh=mesh,
        in_specs=(
            P(BOTH, None),
            P(BOTH, None),
            P(),
            P("expert", None, "hidden"),
            P("expert", "hidden", None),
        ),
        out_specs=(
            P(BOTH, None),
            P("hidden", "expert"),
            P("expert", None, "hidden"),
            P("expert", "hidden", None),
        ),
        check_vma=False,
    )
```

```python
import functools
import math

import jax
import jax.numpy as jnp
from jax import lax
from jax.experimental import pallas as pl
from jax.experimental.pallas import tpu as pltpu
from jax.sharding import PartitionSpec as P

SLOTS = 2
TOK = 196
BOTH = ("expert", "hidden")
F32, BF16 = jnp.float32, jnp.bfloat16
NN = (((1,), (0,)), ((), ()))
NT = (((1,), (1,)), ((), ()))
TN = (((0,), (0,)), ((), ()))


def dot(left, right, dims=NN):
    return lax.dot_general(left, right, dims, preferred_element_type=F32)


def reorder(shape, old_axes, rows):
    out_row = lax.broadcasted_iota(jnp.int32, (rows, 1), 0)
    strides = [1] * len(shape)
    for axis in reversed(range(len(shape) - 1)):
        strides[axis] = strides[axis + 1] * shape[axis + 1]
    source = jnp.zeros_like(out_row)
    rest = out_row
    for axis in reversed(old_axes):
        source = source + lax.rem(rest, shape[axis]) * strides[axis]
        rest = lax.div(rest, shape[axis])
    columns = lax.broadcasted_iota(jnp.int32, (rows, rows), 1)
    return jnp.where(columns == source, 1.0, 0.0).astype(BF16)


def strided(devices, stride):
    if math.gcd(devices, stride) != 1:
        stride = 1
    return [stride * turn % devices for turn in range(devices)]


def halves(n_expert, n_hidden):
    return [
        (first + n_expert // 2 * step) % n_expert * n_hidden + (-step) % n_hidden
        for first in range(n_expert)
        for step in range(n_hidden)
    ]


def orders(n_expert, n_hidden):
    devices = n_expert * n_hidden
    return strided(devices, 19), halves(n_expert, n_hidden), strided(devices, 15)


def places(order):
    return {device: place for place, device in enumerate(order)}


def softmaxes(logits):
    by_token = jnp.exp(logits - jnp.max(logits, axis=1, keepdims=True))
    dispatch = by_token / jnp.sum(by_token, axis=1, keepdims=True)
    by_slot = jnp.exp(logits - jnp.max(logits, axis=0, keepdims=True))
    combine = by_slot / jnp.sum(by_slot, axis=0, keepdims=True)
    return dispatch, combine


def slots_kernel(dims, tokens_hbm, out_grad_hbm, router_hbm, logits_out, sent, *scratch):
    tokens, out_grad, router, sems = scratch
    n_expert, n_hidden, local_slots = dims
    images, _, width = tokens.shape
    place = places(orders(n_expert, n_hidden)[0])
    copies = [
        pltpu.make_async_copy(source, target, sems.at[i])
        for i, (source, target) in enumerate(
            ((tokens_hbm, tokens), (router_hbm, router), (out_grad_hbm, out_grad))
        )
    ]
    for copy in copies:
        copy.start()
    copies[0].wait()
    copies[1].wait()
    for image in range(images):
        logits = dot(router[...], tokens[image].T)
        logits_out[image] = logits
        dispatch, combine = softmaxes(logits)
        slot_in = dot(dispatch.astype(BF16), tokens[image]).astype(BF16)
        if image == 0:
            copies[2].wait()
        slot_grad = dot(combine.astype(BF16), out_grad[image]).astype(BF16)
        for expert in range(n_expert):
            own = slice(expert * local_slots, (expert + 1) * local_slots)
            block = jnp.concatenate([slot_in[own], slot_grad[own]], axis=0)
            for part in range(n_hidden):
                sent[place[expert * n_hidden + part], image] = block


def experts_kernel(dims, received, weight_in, weight_out, parts, rows_out, act_out, d_pre_out, turned_in, turned_out):
    images, local_experts, chunk, order_in, order_out = dims
    devices, per_source, width = received.shape
    source, place = order_in, places(order_out)
    shape = (chunk, images, 2, local_experts, SLOTS)
    size = chunk * per_source
    part = size // (2 * local_experts)
    to_expert = (2, 3, 0, 1, 4)
    order = reorder(shape, to_expert, size)
    for e in range(local_experts):
        turned_out[e] = weight_out[e].T
        turned_in[e] = weight_in[e].T
    moved = tuple(shape[axis] for axis in to_expert)
    back = reorder(moved, tuple(to_expert.index(axis) for axis in range(5)), size)
    for start in range(0, devices, chunk):
        block = received[start : start + chunk].reshape(size, width)
        rows = dot(order, block).astype(BF16)
        base = start // chunk * part
        forwards, backwards = [], []
        for expert in range(local_experts):
            slot_in = rows[expert * part : (expert + 1) * part]
            slot_grad = rows[(local_experts + expert) * part : (local_experts + expert + 1) * part]
            rows_out[0, expert, base : base + part] = slot_in
            rows_out[1, expert, base : base + part] = slot_grad
            pre = dot(slot_in, weight_in[expert])
            d_act = dot(slot_grad, turned_out[expert])
            half = 0.5 * (1.0 + lax.erf(pre * 0.7071067811865476))
            act = (pre * half).astype(BF16)
            slope = half + pre * jnp.exp(-0.5 * pre * pre) * 0.3989422804014327
            d_pre = (d_act * slope).astype(BF16)
            act_out[expert, base : base + part] = act
            d_pre_out[expert, base : base + part] = d_pre
            forwards.append(dot(act, weight_out[expert]).astype(BF16))
            backwards.append(dot(d_pre, turned_in[expert]).astype(BF16))
        results = dot(back, jnp.concatenate(forwards + backwards, axis=0)).astype(BF16)
        results = results.reshape(chunk, per_source, width)
        for row in range(chunk):
            parts[place[source[start + row]]] = results[row]


def weights_kernel(rows, act, d_pre, grad_in, grad_out):
    grad_in[0] = dot(rows[0, 0], d_pre[0], TN).astype(BF16)
    grad_out[0] = dot(act[0], rows[1, 0], TN).astype(BF16)


def images_kernel(dims, logits_in, tokens, out_grad, parts, terms, left_out, right_out):
    n_expert, n_hidden, local_slots = dims
    images, _, width = tokens.shape
    slots = n_expert * local_slots
    place = places(orders(n_expert, n_hidden)[1])
    block = width // n_hidden
    totals = [jnp.zeros((slots, block), F32)] * n_hidden
    for image in range(images):
        dispatch, combine = softmaxes(logits_in[image])
        summed = []
        for expert in range(n_expert):
            held = [parts[place[expert * n_hidden + part], image] for part in range(n_hidden)]
            summed.append(sum(piece.astype(F32) for piece in held))
        summed = jnp.stack(summed)
        slot_out = summed[:, :local_slots].reshape(slots, width).astype(BF16)
        slot_in_grad = summed[:, local_slots:].reshape(slots, width).astype(BF16)
        d_combine = dot(slot_out, out_grad[image].T)
        d_dispatch = dot(slot_in_grad, tokens[image].T)
        from_combine = combine * (d_combine - jnp.sum(combine * d_combine, axis=0, keepdims=True))
        from_dispatch = dispatch * (
            d_dispatch - jnp.sum(dispatch * d_dispatch, axis=1, keepdims=True)
        )
        d_logits = (from_combine + from_dispatch).astype(BF16)
        for part in range(n_hidden):
            columns = tokens[image, :, part * block : (part + 1) * block]
            totals[part] = totals[part] + dot(d_logits, columns)
        left_out[image, :slots] = dispatch.astype(BF16)
        left_out[image, slots:] = d_logits
        right_out[image] = slot_in_grad
    place = places(orders(n_expert, n_hidden)[2])
    for part in range(n_hidden):
        for expert in range(n_expert):
            own = slice(expert * local_slots, (expert + 1) * local_slots)
            terms[place[expert * n_hidden + part]] = totals[part][own].astype(BF16)


def tokens_kernel(left, slot_in_grad, router, token_grad):
    for image in range(left.shape[0]):
        right = jnp.concatenate([slot_in_grad[image], router[...]], axis=0)
        token_grad[image] = dot(left[image], right, TN).astype(BF16)


def exchange(blocks, order):
    return lax.all_to_all(
        blocks, BOTH, split_axis=0, concat_axis=0, tiled=True, axis_index_groups=[order]
    )


def call(kernel, outs, args, flops, **more):
    moved = sum(x.size * x.dtype.itemsize for x in list(outs) + list(args))
    return pl.pallas_call(
        kernel,
        out_shape=outs,
        cost_estimate=pl.CostEstimate(flops=flops, bytes_accessed=moved, transcendentals=0),
        compiler_params=pltpu.CompilerParams(vmem_limit_bytes=40 * 2**20),
        **more,
    )(*args)


def per_device(n_expert, n_hidden, tokens, out_grad, slot_router, weight_in, weight_out):
    width = tokens.shape[1]
    images = tokens.shape[0] // TOK
    local_experts, _, hidden = weight_in.shape
    local_slots = local_experts * SLOTS
    slots = n_expert * local_slots
    devices = n_expert * n_hidden
    per_source = 2 * images * local_slots
    rows = devices * images * SLOTS
    shape = jax.ShapeDtypeStruct
    inputs = tokens.reshape(images, TOK, width)
    out_grads = out_grad.reshape(images, TOK, width)
    router = slot_router.T
    dims = (n_expert, n_hidden, local_slots)
    order = orders(n_expert, n_hidden)

    logits, sent = call(
        functools.partial(slots_kernel, dims),
        (
            shape((images, slots, TOK), F32),
            shape((devices, images, 2 * local_slots, width), BF16),
        ),
        tuple(pltpu.with_memory_space_constraint(x, pltpu.HBM) for x in (inputs, out_grads, router)),
        6 * images * slots * TOK * width,
        in_specs=[pl.BlockSpec(memory_space=pltpu.HBM)] * 3,
        scratch_shapes=[
            pltpu.VMEM(inputs.shape, BF16),
            pltpu.VMEM(out_grads.shape, BF16),
            pltpu.VMEM(router.shape, BF16),
            pltpu.SemaphoreType.DMA((3,)),
        ],
    )
    (sent,) = call(
        lambda given, kept: None,
        (shape(sent.shape, BF16),),
        (sent,),
        8 * local_experts * rows * width * hidden * n_expert,
        in_specs=[pl.BlockSpec(memory_space=pl.ANY)],
        out_specs=[pl.BlockSpec(memory_space=pl.ANY)],
        input_output_aliases={0: 0},
    )
    received = exchange(sent.reshape(devices, per_source, width), order[0])
    chunk = max(c for c in range(1, devices + 1) if devices % c == 0 and c * per_source <= 256)
    parts, slot_rows, act, d_pre = call(
        functools.partial(experts_kernel, (images, local_experts, chunk, *order[:2])),
        (
            shape((devices, per_source, width), BF16),
            shape((2, local_experts, rows, width), BF16),
            shape((local_experts, rows, hidden), BF16),
            shape((local_experts, rows, hidden), BF16),
        ),
        (received, weight_in, weight_out),
        8 * local_experts * rows * width * hidden,
        scratch_shapes=[pltpu.VMEM((local_experts, hidden, width), BF16), pltpu.VMEM((local_experts, width, hidden), BF16)],
    )
    back = exchange(parts, order[1])
    grad_in, grad_out = call(
        weights_kernel,
        (
            shape((local_experts, width, hidden), BF16),
            shape((local_experts, hidden, width), BF16),
        ),
        (slot_rows, act, d_pre),
        4 * local_experts * rows * width * hidden,
        grid=(local_experts,),
        in_specs=[
            pl.BlockSpec((2, 1, rows, width), lambda e: (0, e, 0, 0)),
            pl.BlockSpec((1, rows, hidden), lambda e: (e, 0, 0)),
            pl.BlockSpec((1, rows, hidden), lambda e: (e, 0, 0)),
        ],
        out_specs=[
            pl.BlockSpec((1, width, hidden), lambda e: (e, 0, 0)),
            pl.BlockSpec((1, hidden, width), lambda e: (e, 0, 0)),
        ],
    )
    terms, left, slot_in_grad = call(
        functools.partial(images_kernel, dims),
        (
            shape((devices, local_slots, width // n_hidden), BF16),
            shape((images, 2 * slots, TOK), BF16),
            shape((images, slots, width), BF16),
        ),
        (
            logits,
            inputs,
            out_grads,
            back.reshape(devices, images, 2 * local_slots, width),
        ),
        6 * images * slots * TOK * width,
    )
    (token_grad,) = call(
        tokens_kernel,
        (shape((images, TOK, width), BF16),),
        (left, slot_in_grad, router),
        4 * images * slots * TOK * width,
    )
    router_parts = exchange(terms, order[2])
    router_grad = jnp.sum(router_parts.astype(F32), axis=0).T
    return token_grad.reshape(images * TOK, width), router_grad, grad_in, grad_out


def solution(mesh):
    return jax.shard_map(
        functools.partial(per_device, mesh.shape["expert"], mesh.shape["hidden"]),
        mesh=mesh,
        in_specs=(
            P(BOTH, None),
            P(BOTH, None),
            P(),
            P("expert", None, "hidden"),
            P("expert", "hidden", None),
        ),
        out_specs=(
            P(BOTH, None),
            P("hidden", "expert"),
            P("expert", None, "hidden"),
            P("expert", "hidden", None),
        ),
        check_vma=False,
    )
```

```python
import functools
import math

import jax
import jax.numpy as jnp
from jax import lax
from jax.experimental import pallas as pl
from jax.experimental.pallas import tpu as pltpu
from jax.sharding import PartitionSpec as P

SLOTS = 2
TOK = 196
BOTH = ("expert", "hidden")
F32, BF16 = jnp.float32, jnp.bfloat16
NN = (((1,), (0,)), ((), ()))
NT = (((1,), (1,)), ((), ()))
TN = (((0,), (0,)), ((), ()))


def dot(left, right, dims=NN):
    return lax.dot_general(left, right, dims, preferred_element_type=F32)


def reorder(shape, old_axes, rows):
    out_row = lax.broadcasted_iota(jnp.int32, (rows, 1), 0)
    strides = [1] * len(shape)
    for axis in reversed(range(len(shape) - 1)):
        strides[axis] = strides[axis + 1] * shape[axis + 1]
    source = jnp.zeros_like(out_row)
    rest = out_row
    for axis in reversed(old_axes):
        source = source + lax.rem(rest, shape[axis]) * strides[axis]
        rest = lax.div(rest, shape[axis])
    columns = lax.broadcasted_iota(jnp.int32, (rows, rows), 1)
    return jnp.where(columns == source, 1.0, 0.0).astype(BF16)


def strided(devices, stride):
    if math.gcd(devices, stride) != 1:
        stride = 1
    return [stride * turn % devices for turn in range(devices)]


def halves(n_expert, n_hidden):
    return [
        (first + n_expert // 2 * step) % n_expert * n_hidden + (-step) % n_hidden
        for first in range(n_expert)
        for step in range(n_hidden)
    ]


def orders(n_expert, n_hidden):
    devices = n_expert * n_hidden
    return strided(devices, 19), halves(n_expert, n_hidden), strided(devices, 15)


def places(order):
    return {device: place for place, device in enumerate(order)}


def softmaxes(logits):
    by_token = jnp.exp(logits - jnp.max(logits, axis=1, keepdims=True))
    dispatch = by_token / jnp.sum(by_token, axis=1, keepdims=True)
    by_slot = jnp.exp(logits - jnp.max(logits, axis=0, keepdims=True))
    combine = by_slot / jnp.sum(by_slot, axis=0, keepdims=True)
    return dispatch, combine


def slots_kernel(dims, tokens, out_grad, router, logits_out, sent):
    n_expert, n_hidden, local_slots = dims
    images, _, width = tokens.shape
    place = places(orders(n_expert, n_hidden)[0])
    for image in range(images):
        logits = dot(router[...], tokens[image].T)
        logits_out[image] = logits
        dispatch, combine = softmaxes(logits)
        slot_in = dot(dispatch.astype(BF16), tokens[image]).astype(BF16)
        slot_grad = dot(combine.astype(BF16), out_grad[image]).astype(BF16)
        for expert in range(n_expert):
            own = slice(expert * local_slots, (expert + 1) * local_slots)
            block = jnp.concatenate([slot_in[own], slot_grad[own]], axis=0)
            for part in range(n_hidden):
                sent[place[expert * n_hidden + part], image] = block


def experts_kernel(dims, received, weight_in, weight_out, parts, rows_out, act_out, d_pre_out, turned_in, turned_out):
    images, local_experts, chunk, order_in, order_out = dims
    devices, per_source, width = received.shape
    source, place = order_in, places(order_out)
    shape = (chunk, images, 2, local_experts, SLOTS)
    size = chunk * per_source
    part = size // (2 * local_experts)
    to_expert = (2, 3, 0, 1, 4)
    order = reorder(shape, to_expert, size)
    for e in range(local_experts):
        turned_out[e] = weight_out[e].T
        turned_in[e] = weight_in[e].T
    moved = tuple(shape[axis] for axis in to_expert)
    back = reorder(moved, tuple(to_expert.index(axis) for axis in range(5)), size)
    for start in range(0, devices, chunk):
        block = received[start : start + chunk].reshape(size, width)
        rows = dot(order, block).astype(BF16)
        base = start // chunk * part
        forwards, backwards = [], []
        for expert in range(local_experts):
            slot_in = rows[expert * part : (expert + 1) * part]
            slot_grad = rows[(local_experts + expert) * part : (local_experts + expert + 1) * part]
            rows_out[0, expert, base : base + part] = slot_in
            rows_out[1, expert, base : base + part] = slot_grad
            pre = dot(slot_in, weight_in[expert])
            d_act = dot(slot_grad, turned_out[expert])
            half = 0.5 * (1.0 + lax.erf(pre * 0.7071067811865476))
            act = (pre * half).astype(BF16)
            slope = half + pre * jnp.exp(-0.5 * pre * pre) * 0.3989422804014327
            d_pre = (d_act * slope).astype(BF16)
            act_out[expert, base : base + part] = act
            d_pre_out[expert, base : base + part] = d_pre
            forwards.append(dot(act, weight_out[expert]).astype(BF16))
            backwards.append(dot(d_pre, turned_in[expert]).astype(BF16))
        results = dot(back, jnp.concatenate(forwards + backwards, axis=0)).astype(BF16)
        results = results.reshape(chunk, per_source, width)
        for row in range(chunk):
            parts[place[source[start + row]]] = results[row]


def weights_kernel(rows, act, d_pre, grad_in, grad_out):
    grad_in[0] = dot(rows[0, 0], d_pre[0], TN).astype(BF16)
    grad_out[0] = dot(act[0], rows[1, 0], TN).astype(BF16)


def images_kernel(dims, logits_in, tokens, out_grad, parts, terms, left_out, right_out):
    n_expert, n_hidden, local_slots = dims
    images, _, width = tokens.shape
    slots = n_expert * local_slots
    place = places(orders(n_expert, n_hidden)[1])
    block = width // n_hidden
    totals = [jnp.zeros((slots, block), F32)] * n_hidden
    for image in range(images):
        dispatch, combine = softmaxes(logits_in[image])
        summed = []
        for expert in range(n_expert):
            held = [parts[place[expert * n_hidden + part], image] for part in range(n_hidden)]
            summed.append(sum(piece.astype(F32) for piece in held))
        summed = jnp.stack(summed)
        slot_out = summed[:, :local_slots].reshape(slots, width).astype(BF16)
        slot_in_grad = summed[:, local_slots:].reshape(slots, width).astype(BF16)
        d_combine = dot(slot_out, out_grad[image].T)
        d_dispatch = dot(slot_in_grad, tokens[image].T)
        from_combine = combine * (d_combine - jnp.sum(combine * d_combine, axis=0, keepdims=True))
        from_dispatch = dispatch * (
            d_dispatch - jnp.sum(dispatch * d_dispatch, axis=1, keepdims=True)
        )
        d_logits = (from_combine + from_dispatch).astype(BF16)
        for part in range(n_hidden):
            columns = tokens[image, :, part * block : (part + 1) * block]
            totals[part] = totals[part] + dot(d_logits, columns)
        left_out[image, :slots] = dispatch.astype(BF16)
        left_out[image, slots:] = d_logits
        right_out[image] = slot_in_grad
    place = places(orders(n_expert, n_hidden)[2])
    for part in range(n_hidden):
        for expert in range(n_expert):
            own = slice(expert * local_slots, (expert + 1) * local_slots)
            terms[place[expert * n_hidden + part]] = totals[part][own].astype(BF16)


def tokens_kernel(left, slot_in_grad, router, token_grad):
    for image in range(left.shape[0]):
        right = jnp.concatenate([slot_in_grad[image], router[...]], axis=0)
        token_grad[image] = dot(left[image], right, TN).astype(BF16)


def exchange(blocks, order):
    return lax.all_to_all(
        blocks, BOTH, split_axis=0, concat_axis=0, tiled=True, axis_index_groups=[order]
    )


def call(kernel, outs, args, flops, **more):
    moved = sum(x.size * x.dtype.itemsize for x in list(outs) + list(args))
    return pl.pallas_call(
        kernel,
        out_shape=outs,
        cost_estimate=pl.CostEstimate(flops=flops, bytes_accessed=moved, transcendentals=0),
        compiler_params=pltpu.CompilerParams(vmem_limit_bytes=40 * 2**20),
        **more,
    )(*args)


def per_device(n_expert, n_hidden, tokens, out_grad, slot_router, weight_in, weight_out):
    width = tokens.shape[1]
    images = tokens.shape[0] // TOK
    local_experts, _, hidden = weight_in.shape
    local_slots = local_experts * SLOTS
    slots = n_expert * local_slots
    devices = n_expert * n_hidden
    per_source = 2 * images * local_slots
    rows = devices * images * SLOTS
    shape = jax.ShapeDtypeStruct
    inputs = tokens.reshape(images, TOK, width)
    out_grads = out_grad.reshape(images, TOK, width)
    router = slot_router.T
    dims = (n_expert, n_hidden, local_slots)
    order = orders(n_expert, n_hidden)

    logits, sent = call(
        functools.partial(slots_kernel, dims),
        (
            shape((images, slots, TOK), F32),
            shape((devices, images, 2 * local_slots, width), BF16),
        ),
        tuple(pltpu.with_memory_space_constraint(x, pltpu.HBM) for x in (inputs, out_grads, router)),
        6 * images * slots * TOK * width,
    )
    (sent,) = call(
        lambda given, kept: None,
        (shape(sent.shape, BF16),),
        (sent,),
        8 * local_experts * rows * width * hidden * n_expert,
        in_specs=[pl.BlockSpec(memory_space=pl.ANY)],
        out_specs=[pl.BlockSpec(memory_space=pl.ANY)],
        input_output_aliases={0: 0},
    )
    received = exchange(sent.reshape(devices, per_source, width), order[0])
    chunk = max(c for c in range(1, devices + 1) if devices % c == 0 and c * per_source <= 256)
    parts, slot_rows, act, d_pre = call(
        functools.partial(experts_kernel, (images, local_experts, chunk, *order[:2])),
        (
            shape((devices, per_source, width), BF16),
            shape((2, local_experts, rows, width), BF16),
            shape((local_experts, rows, hidden), BF16),
            shape((local_experts, rows, hidden), BF16),
        ),
        (received, weight_in, weight_out),
        8 * local_experts * rows * width * hidden,
        scratch_shapes=[pltpu.VMEM((local_experts, hidden, width), BF16), pltpu.VMEM((local_experts, width, hidden), BF16)],
    )
    back = exchange(parts, order[1])
    grad_in, grad_out = call(
        weights_kernel,
        (
            shape((local_experts, width, hidden), BF16),
            shape((local_experts, hidden, width), BF16),
        ),
        (slot_rows, act, d_pre),
        4 * local_experts * rows * width * hidden,
        grid=(local_experts,),
        in_specs=[
            pl.BlockSpec((2, 1, rows, width), lambda e: (0, e, 0, 0)),
            pl.BlockSpec((1, rows, hidden), lambda e: (e, 0, 0)),
            pl.BlockSpec((1, rows, hidden), lambda e: (e, 0, 0)),
        ],
        out_specs=[
            pl.BlockSpec((1, width, hidden), lambda e: (e, 0, 0)),
            pl.BlockSpec((1, hidden, width), lambda e: (e, 0, 0)),
        ],
    )
    terms, left, slot_in_grad = call(
        functools.partial(images_kernel, dims),
        (
            shape((devices, local_slots, width // n_hidden), BF16),
            shape((images, 2 * slots, TOK), BF16),
            shape((images, slots, width), BF16),
        ),
        (
            logits,
            inputs,
            out_grads,
            back.reshape(devices, images, 2 * local_slots, width),
        ),
        6 * images * slots * TOK * width,
    )
    (token_grad,) = call(
        tokens_kernel,
        (shape((images, TOK, width), BF16),),
        (left, slot_in_grad, router),
        4 * images * slots * TOK * width,
    )
    router_parts = exchange(terms, order[2])
    router_grad = jnp.sum(router_parts.astype(F32), axis=0).T
    return token_grad.reshape(images * TOK, width), router_grad, grad_in, grad_out


def solution(mesh):
    return jax.shard_map(
        functools.partial(per_device, mesh.shape["expert"], mesh.shape["hidden"]),
        mesh=mesh,
        in_specs=(
            P(BOTH, None),
            P(BOTH, None),
            P(),
            P("expert", None, "hidden"),
            P("expert", "hidden", None),
        ),
        out_specs=(
            P(BOTH, None),
            P("hidden", "expert"),
            P("expert", None, "hidden"),
            P("expert", "hidden", None),
        ),
        check_vma=False,
    )
```
